32 devices in a mesh: group: 1, ep: 32 (over z, y, x, core), sub: 1.
Axes of the slice: x: 2, y: 2, z: 4, core: 2. Of those that a mesh axis runs over, the one named last changes fastest.
Arguments:
- hidden: bfloat16 [256, 4096], P(('group', 'ep', 'sub')), may hold values from -6 to 6
- query: bfloat16 [256, 4096], P(('group', 'ep', 'sub')), may hold values from -120 to 120
- cached_key_store: bfloat16 [256, 32, 256], P(('group', 'ep', 'sub')), may hold values from -4.5 to 4.5
- cached_value_store: bfloat16 [256, 32, 256], P(('group', 'ep', 'sub')), may hold values from -9 to 9
- current_key: bfloat16 [256, 256], P(('group', 'ep', 'sub')), may hold values from -6 to 6
- current_value: bfloat16 [256, 256], P(('group', 'ep', 'sub')), may hold values from -9 to 9
- norm_gain: float32 [4096], replicated, may hold values from 0.1 to 1.9
- expert_ids: int32 [256, 8], P(('group', 'ep')), may hold values from 0 to 15, all different within a row; in each aligned block of 8 rows (0 to 7, 8 to 15, ...) at most 4 rows name the same one
- gate_weights: float32 [256, 8], P(('group', 'ep')), may hold values from 0.05 to 0.35
- w_gate: bfloat16 [32, 4096, 384], P('ep', None, 'sub'), may hold values from -0.09375 to 0.09375
- w_up: bfloat16 [32, 4096, 384], P('ep', None, 'sub'), may hold values from -0.09375 to 0.09375
- w_down: bfloat16 [32, 384, 4096], P('ep', None, 'sub'), may hold values from -0.21875 to 0.21875
Outputs:
- ffn_out: bfloat16 [256, 4096], P(('group', 'ep'), 'sub')
The draws below stay inside these ranges and needn't reach their ends.
Inputs may be any that keep to these rules, and one draw needn't show every extreme that they name: `expert_ids`: each token names 8 different experts; within the rows of one device (aligned blocks of 8 rows) no expert is named by more than 4 rows, a bound that some block reaches.
All inputs are finite; a program needn't handle non-finite values.
Results may differ from the reference program's by a relative error of at most 0.019.
Values may be sent and summed in bfloat16 or wider, within the bound.
A program may use at most 64 MiB of HBM per device.

```python
import math
import jax
import jax.numpy as jnp
import numpy as np
from jax import lax

D = 4096
QUERY_HEADS = 32
KEY_VALUE_HEADS = 2
HEAD_SIZE = 128
FF = 768
TOP = 8
REQ_DEV = 8
CACHED_POSITIONS = 32
EXPERTS = 16
SLICE_FF = 384
CAP = 4
REQUEST_COUNT = 256
N_EP = 32


def base_keys(key):
    normalized_keys = jax.random.normal(jax.random.fold_in(key, 101), (REQUEST_COUNT, CACHED_POSITIONS, KEY_VALUE_HEADS * HEAD_SIZE), jnp.float32)
    return jnp.clip(normalized_keys, -4.5, 4.5)


def draw_cached_key_store(key, part):
    shared_heads = base_keys(key)
    return shared_heads.astype(jnp.bfloat16)


def draw_query(key, part):
    key = jax.random.fold_in(key, 2)
    fresh = jax.random.normal(key, (REQUEST_COUNT, QUERY_HEADS * HEAD_SIZE), jnp.float32)
    fresh = jnp.clip(fresh, -6.0, 6.0)
    return fresh.astype(jnp.bfloat16)


def block_levels(rng, dims, cuts, least, top_value):
    gain = 1.0
    for position, parts in cuts:
        draws = jax.random.uniform(jax.random.fold_in(jax.random.fold_in(rng, 6), position), (parts,), jnp.float32, least / len(cuts), top_value / len(cuts))
        gain = gain * jnp.repeat(jnp.exp(draws), dims[position] // parts).reshape((-1,) + (1,) * (len(dims) - 1 - position))
    return gain


def routed_block(stream_key, own, number, rows, amount, top, bound, lean):
    order = jax.random.permutation(stream_key, amount)
    packed, usual = load_shares(amount, rows * top, bound, lean, True), load_shares(amount, rows * top, bound, lean, False)
    places = jnp.arange(amount)

    def named(tallies, turn):
        used = int((tallies > 0).sum())
        fixed = max(1, used // 4)
        shifted = fixed + (places - fixed + turn * (used - fixed)) % max(1, amount - fixed)
        return jnp.zeros((amount,), jnp.int32).at[order[jnp.where(places < fixed, places, shifted)]].set(jnp.asarray(tallies, jnp.int32))

    tallies = jnp.where(number % 4 == 0, named(packed, number // 4), named(usual, number - number // 4 - 1))
    mixed = jax.random.permutation(jax.random.fold_in(own, 3), amount)
    source_of, sink = mixed[0:amount // 2 * 2:2], mixed[1:amount // 2 * 2:2]
    room = jnp.minimum(tallies[source_of] - 1, bound - tallies[sink]) // 2
    room = jnp.where((source_of == order[0]) | (sink == order[0]) | (tallies[sink] == 0), 0, jnp.maximum(room, 0))
    shifted = jax.random.randint(jax.random.fold_in(own, 4), (amount // 2,), 0, 1 << 20) % (room + 1)
    tallies = tallies.at[source_of].add(-shifted).at[sink].add(shifted)
    items = jnp.searchsorted(jnp.cumsum(tallies), jnp.arange(rows * top), side="right").astype(jnp.int32)
    grid = items.reshape(top, rows).T
    grid = grid[jax.random.permutation(jax.random.fold_in(own, 1), rows)]
    turn = jax.random.randint(jax.random.fold_in(own, 2), (rows, 1), 0, top)
    return jnp.take_along_axis(grid, (jnp.arange(top)[None, :] + turn) % top, axis=1)


def load_shares(amount, total, reach, slope, full):
    portions = [(1 << 20) // math.isqrt(grade ** slope) + 1 for grade in range(1, amount + 1)]
    largest = reach if full else min(reach, max(-(-total // amount), total * portions[0] // sum(portions)))
    least = 1 if total - largest >= amount - 1 else 0
    given, rest = [largest] + [least] * (amount - 1), total - largest - least * (amount - 1)
    while rest > 0:
        movable = [i for i in range(1, amount) if given[i] < largest] or [i for i in range(1, amount) if given[i] < reach]
        mass, remaining = sum([portions[i] for i in movable]), rest
        for i in movable:
            extra = min(reach - given[i], max(1, remaining * portions[i] // mass), rest)
            given[i] = given[i] + extra
            rest = rest - extra
    return np.array(given)


def noise(own_key, shape, deviation, reach, pieces=(), kind=jnp.bfloat16):
    entries = jax.random.normal(own_key, shape, jnp.float32) * deviation
    if len(pieces) > 0:
        entries = block_levels(own_key, shape, pieces, -0.22, 0.18) * entries
    return jnp.clip(entries, min=-reach, max=reach).astype(kind)


def setup_inputs(seed: int = 0, part: int = 0) -> dict:
    seeds = jax.random.split(jax.random.key(seed), 13)
    own_keys = jax.random.split(jax.random.fold_in(seeds[12], part), 13)
    hidden = noise(own_keys[0], (REQUEST_COUNT, D), 1.0, 6.0, ((0, 32),))
    query = draw_query(jax.random.fold_in(jax.random.fold_in(seeds[12], part), 71), part)
    cached_key_store = draw_cached_key_store(jax.random.fold_in(jax.random.fold_in(seeds[12], part), 71), part)
    cached_value_store = noise(own_keys[3], (REQUEST_COUNT, CACHED_POSITIONS, KEY_VALUE_HEADS * HEAD_SIZE), 1.5, 9.0, ((0, 32),))
    current_key = noise(own_keys[4], (REQUEST_COUNT, KEY_VALUE_HEADS * HEAD_SIZE), 1.0, 6.0, ((0, 32),))
    current_value = noise(own_keys[5], (REQUEST_COUNT, KEY_VALUE_HEADS * HEAD_SIZE), 1.5, 9.0, ((0, 32),))
    norm_gain = jnp.clip(1.0 + 0.18 * jax.random.normal(seeds[6], (D,), jnp.float32), 0.1, 1.9)
    expert_ids_keys = jax.random.split(jax.random.fold_in(own_keys[7], 1), REQUEST_COUNT // REQ_DEV)
    expert_ids_turns = jax.random.permutation(jax.random.fold_in(own_keys[7], 3), REQUEST_COUNT // REQ_DEV)
    expert_ids = jax.vmap(lambda own, number: routed_block(jax.random.fold_in(own_keys[7], 2), own, number, REQ_DEV, EXPERTS, TOP, CAP, 2))(expert_ids_keys, expert_ids_turns).reshape((REQUEST_COUNT, TOP))
    gate_weights = jnp.clip(0.05 + 0.29999999 * jax.random.uniform(own_keys[8], (REQUEST_COUNT, TOP), jnp.float32) ** block_levels(own_keys[8], (REQUEST_COUNT, TOP), ((0, 32),), -0.2, 0.2), 0.05, 0.35)
    w_gate = noise(seeds[9], (N_EP, D, SLICE_FF), D ** -0.5, 0.09375, ((0, 32),))
    w_up = noise(seeds[10], (N_EP, D, SLICE_FF), D ** -0.5, 0.09375, ((0, 32),))
    w_down = noise(seeds[11], (N_EP, SLICE_FF, D), FF ** -0.5, 0.21875, ((0, 32),))
    return dict(hidden=hidden, query=query, cached_key_store=cached_key_store, cached_value_store=cached_value_store, current_key=current_key, current_value=current_value, norm_gain=norm_gain, expert_ids=expert_ids, gate_weights=gate_weights, w_gate=w_gate, w_up=w_up, w_down=w_down)


epsilon = 1e-06

def attend_norm(hidden, query, cached_key_store, cached_value_store, current_key, current_value, norm_gain):
    token_list = hidden.shape[0]
    query_group_width = QUERY_HEADS // KEY_VALUE_HEADS
    scaling = 1.0 / math.sqrt(HEAD_SIZE)
    key_row_block = jnp.concatenate([cached_key_store, current_key[:, None, :]], axis=1).astype(jnp.float32).reshape(token_list, CACHED_POSITIONS + 1, KEY_VALUE_HEADS, HEAD_SIZE)
    value_row_block = jnp.concatenate([cached_value_store, current_value[:, None, :]], axis=1).astype(jnp.float32).reshape(token_list, CACHED_POSITIONS + 1, KEY_VALUE_HEADS, HEAD_SIZE)
    query_rows = query.astype(jnp.float32).reshape(token_list, KEY_VALUE_HEADS, query_group_width, HEAD_SIZE)
    scores = jnp.einsum('tgqd,tpgd->tgqp', query_rows, key_row_block) * scaling
    probs = jax.nn.softmax(scores, axis=-1).astype(jnp.bfloat16)
    attended = jnp.einsum('tgqp,tpgd->tgqd', probs.astype(jnp.float32), value_row_block).reshape(token_list, QUERY_HEADS * HEAD_SIZE)
    resid = hidden.astype(jnp.float32) + attended
    meansq = lax.optimization_barrier(jnp.mean(resid * resid, axis=-1, keepdims=True))
    return (resid * lax.rsqrt(meansq + epsilon) * norm_gain).astype(jnp.bfloat16)

def reference(hidden, query, cached_key_store, cached_value_store, current_key, current_value, norm_gain, expert_ids, gate_weights, w_gate, w_up, w_down):
    token_list = hidden.shape[0]
    normed = attend_norm(hidden, query, cached_key_store, cached_value_store, current_key, current_value, norm_gain)
    spread = N_EP // EXPERTS
    blocks = token_list // REQ_DEV
    block_picks = REQ_DEV * TOP
    chosen = expert_ids.reshape(blocks, block_picks)
    weights_flat = gate_weights.reshape(blocks, block_picks)
    onehot = (chosen[:, :, None] == jnp.arange(EXPERTS, dtype=jnp.int32)[None, None, :]).astype(jnp.int32)
    slot_rank = lax.optimization_barrier(jnp.sum((jnp.cumsum(onehot, axis=1) - onehot) * onehot, axis=2))
    target = chosen * CAP + slot_rank
    columns = jnp.arange(EXPERTS * CAP, dtype=jnp.int32)
    match = target[:, None, :] == columns[None, :, None]
    live_slot = jnp.any(match, axis=2)
    pick_index = jnp.arange(block_picks, dtype=jnp.int32)
    owner_row = lax.optimization_barrier(jnp.sum(jnp.where(match, pick_index[None, None, :], 0), axis=2)).astype(jnp.int32)
    token_index = jnp.arange(blocks, dtype=jnp.int32)[:, None] * REQ_DEV + owner_row // TOP
    slot_weight = jnp.where(live_slot, jnp.take_along_axis(weights_flat, owner_row, axis=1), 0.0)
    token_by_expert = token_index.reshape(blocks, EXPERTS, CAP).transpose(1, 0, 2).reshape(EXPERTS, blocks * CAP)
    weight_by_expert = slot_weight.reshape(blocks, EXPERTS, CAP).transpose(1, 0, 2).reshape(EXPERTS, blocks * CAP)

    def one_slice(running, inputs):
        gate_slice, up_slice, down_slice, slice_index = inputs
        expert = slice_index // spread
        rows_index = token_by_expert[expert]
        weight_row = weight_by_expert[expert]
        gathered = normed[rows_index]
        gated = jnp.dot(gathered, gate_slice, preferred_element_type=jnp.float32)
        raised = jnp.dot(gathered, up_slice, preferred_element_type=jnp.float32)
        activated = (jax.nn.silu(gated) * raised).astype(jnp.bfloat16)
        partial_rows = jnp.dot(activated, down_slice, preferred_element_type=jnp.float32).astype(jnp.bfloat16)
        running = running + jax.ops.segment_sum(partial_rows.astype(jnp.float32) * weight_row[:, None], rows_index, num_segments=token_list)
        return (running, None)
    start_value = jnp.zeros((token_list, D), jnp.float32)
    running = lax.scan(one_slice, start_value, (w_gate, w_up, w_down, jnp.arange(N_EP, dtype=jnp.int32)))[0]
    return running.astype(jnp.bfloat16)
```

```python
import functools
import math

import jax
import jax.numpy as jnp
from jax import lax
from jax.experimental import pallas as pl
from jax.experimental.pallas import tpu as pltpu
from jax.sharding import PartitionSpec as P

QUERY_HEADS = 32
KEY_VALUE_HEADS = 2
HEAD_SIZE = 128
FF = 768


epsilon = 1e-06


def attend_norm(
    hidden, query, cached_key_store, cached_value_store, current_key, current_value, norm_gain
):
    count_of_rows = hidden.shape[0]
    context_output = cached_key_store.shape[1]
    query_group_width = QUERY_HEADS // KEY_VALUE_HEADS
    scaling = 1.0 / math.sqrt(HEAD_SIZE)
    query_rows = query.reshape(count_of_rows, KEY_VALUE_HEADS, query_group_width, HEAD_SIZE)
    key_row_block = cached_key_store.reshape(
        count_of_rows, context_output, KEY_VALUE_HEADS, HEAD_SIZE
    )
    value_row_block = cached_value_store.reshape(
        count_of_rows, context_output, KEY_VALUE_HEADS, HEAD_SIZE
    )
    incoming_key = current_key.reshape(count_of_rows, KEY_VALUE_HEADS, HEAD_SIZE)
    incoming_value = current_value.reshape(count_of_rows, KEY_VALUE_HEADS, HEAD_SIZE)
    old_scores = (
        jnp.einsum("tgqd,tpgd->tgqp", query_rows, key_row_block, preferred_element_type=jnp.float32)
        * scaling
    )
    new_scores = (
        jnp.einsum("tgqd,tgd->tgq", query_rows, incoming_key, preferred_element_type=jnp.float32)
        * scaling
    )
    top_score = jnp.maximum(jnp.max(old_scores, axis=-1), new_scores)
    old_exp = jnp.exp(old_scores - top_score[..., None])
    new_exp = jnp.exp(new_scores - top_score)
    denominator = jnp.sum(old_exp, axis=-1) + new_exp
    old_probs = (old_exp / denominator[..., None]).astype(jnp.bfloat16)
    new_probs = (new_exp / denominator).astype(jnp.bfloat16)
    attended = jnp.einsum(
        "tgqp,tpgd->tgqd", old_probs, value_row_block, preferred_element_type=jnp.float32
    )
    attended = (
        attended
        + new_probs.astype(jnp.float32)[..., None]
        * incoming_value.astype(jnp.float32)[:, :, None, :]
    )
    resid = hidden.astype(jnp.float32) + attended.reshape(count_of_rows, QUERY_HEADS * HEAD_SIZE)
    meansq = jnp.mean(resid * resid, axis=-1, keepdims=True)
    return (resid * lax.rsqrt(meansq + epsilon) * norm_gain).astype(jnp.bfloat16)


def slot_targets(chosen, experts, capacity):
    flattened = chosen.reshape(-1)
    onehot = (flattened[:, None] == jnp.arange(experts, dtype=jnp.int32)[None, :]).astype(jnp.int32)
    slot_rank = jnp.sum((jnp.cumsum(onehot, axis=0) - onehot) * onehot, axis=1)
    return (flattened * capacity + slot_rank).reshape(chosen.shape)


def pack_rows(normed, target, experts, capacity, spread):
    model_width = normed.shape[1]
    all_slots = jnp.arange(experts * capacity, dtype=jnp.int32)
    match = all_slots[:, None, None] == target[None, :, :]
    picker = jnp.any(match, axis=2).astype(jnp.bfloat16)
    packed = jnp.dot(picker, normed, preferred_element_type=jnp.float32).astype(jnp.bfloat16)
    packed = packed.reshape(experts, 1, capacity, model_width)
    widened = jnp.broadcast_to(packed, (experts, spread, capacity, model_width))
    return widened.reshape(experts * spread, capacity, model_width)


def expert_hidden(slot_rows, w_gate, w_up):
    flattened = slot_rows.reshape(-1, slot_rows.shape[-1])
    gated = jnp.dot(flattened, w_gate[0], preferred_element_type=jnp.float32)
    raised = jnp.dot(flattened, w_up[0], preferred_element_type=jnp.float32)
    activated = (jax.nn.silu(gated) * raised).astype(jnp.bfloat16)
    return activated.reshape(slot_rows.shape[:-1] + (activated.shape[1],))


def expert_down(activated, w_down):
    out_width = w_down.shape[2]
    portion = lax.all_gather(activated, "sub", axis=3, tiled=True)
    unit_rows = portion.reshape(-1, portion.shape[-1])
    unit_weights = w_down[0]
    running = jnp.dot(unit_rows, unit_weights, preferred_element_type=jnp.float32)
    return running.astype(jnp.bfloat16).reshape(activated.shape[:3] + (out_width,))


def moe_block(
    normed, ids_pair, gates_pair, w_gate, w_up, w_down, experts, spread, capacity, sub_place
):
    pair_count = ids_pair.shape[0]
    count_of_rows = ids_pair.shape[1]
    targets = jnp.stack(
        [slot_targets(ids_pair[side], experts, capacity) for side in range(pair_count)]
    )
    own_targets = lax.dynamic_index_in_dim(targets, sub_place, 0, keepdims=False)
    outgoing = pack_rows(normed, own_targets, experts, capacity, spread)
    arrived = lax.all_to_all(outgoing, "ep", split_axis=0, concat_axis=0, tiled=True)
    activated = expert_hidden(
        lax.all_gather(arrived[None], "sub", axis=0, tiled=True), w_gate, w_up
    )
    partial_rows = expert_down(activated, w_down)
    returned = lax.all_to_all(partial_rows, "ep", split_axis=1, concat_axis=1, tiled=True)
    shaped = returned.reshape(pair_count, experts, spread, capacity, returned.shape[3])
    summed = jnp.sum(shaped, axis=2, dtype=jnp.float32)
    contract = "snec,sech->snh"
    columns = jnp.arange(experts * capacity, dtype=jnp.int32)
    selected = (targets[..., None] == columns).astype(jnp.float32)
    mixing = jnp.einsum("snk,snkc->snc", gates_pair, selected, precision=lax.Precision.HIGHEST)
    mixing = mixing.reshape(pair_count, count_of_rows, experts, capacity)
    return jnp.einsum(contract, mixing, summed, precision=lax.Precision.HIGHEST).astype(
        jnp.bfloat16
    )


CAPACITY = 4
ROWS = 8
BLOCK = 16
PARTS = 2
F32 = jnp.float32
BF16 = jnp.bfloat16


def attention_rows(hidden_ref, query_ref, keys_ref, values_ref, new_key_ref, new_value_ref, gain_ref):
    positions = keys_ref.shape[1]
    group = QUERY_HEADS // KEY_VALUE_HEADS
    scaling = 1.0 / math.sqrt(HEAD_SIZE)
    query = query_ref[...].astype(F32)
    rows, columns = group * ROWS, ROWS * positions
    row_token = lax.broadcasted_iota(jnp.int32, (rows, columns), 0) % ROWS
    column_token = lax.broadcasted_iota(jnp.int32, (rows, columns), 1) // positions
    own = row_token == column_token
    pieces = []
    for g in range(KEY_VALUE_HEADS):
        lanes = slice(g * HEAD_SIZE, (g + 1) * HEAD_SIZE)
        stacked = jnp.concatenate(
            [
                query[:, (g * group + h) * HEAD_SIZE : (g * group + h + 1) * HEAD_SIZE]
                for h in range(group)
            ],
            axis=0,
        )
        keys = keys_ref[:, :, lanes].reshape(columns, HEAD_SIZE)
        values = values_ref[:, :, lanes].reshape(columns, HEAD_SIZE)
        scores = lax.dot_general(
            stacked.astype(BF16), keys, (((1,), (1,)), ((), ())), preferred_element_type=F32
        )
        scores = jnp.where(own, scores * scaling, -1e30)
        new_key = jnp.concatenate([new_key_ref[:, lanes].astype(F32)] * group, axis=0)
        new_value = jnp.concatenate([new_value_ref[:, lanes].astype(F32)] * group, axis=0)
        new_score = jnp.sum(stacked * new_key, axis=1, keepdims=True) * scaling
        top = jnp.maximum(jnp.max(scores, axis=1, keepdims=True), new_score)
        weights = jnp.exp(scores - top)
        new_weight = jnp.exp(new_score - top)
        total = jnp.sum(weights, axis=1, keepdims=True) + new_weight
        probs = (weights / total).astype(BF16)
        new_prob = (new_weight / total).astype(BF16).astype(F32)
        attended = jnp.dot(probs, values, preferred_element_type=F32) + new_prob * new_value
        pieces += [attended[h * ROWS : (h + 1) * ROWS] for h in range(group)]
    resid = hidden_ref[...].astype(F32) + jnp.concatenate(pieces, axis=1)
    meansq = jnp.mean(resid * resid, axis=1, keepdims=True)
    return resid * lax.rsqrt(meansq + epsilon) * gain_ref[...]


def slot_weights(ids_ref, gates_ref, chips, my_chip):
    slots = chips * BLOCK
    place = lax.broadcasted_iota(jnp.int32, (ROWS, slots), 1)
    token = lax.broadcasted_iota(jnp.int32, (ROWS, slots), 0)
    expert = (place // BLOCK + my_chip) % chips
    quarter = 2 * ((place // 8) % 2) + ((place // 4) % 2 + (place // BLOCK) % 2) % 2
    chosen = jnp.zeros((ROWS, slots), F32)
    weight = jnp.zeros((ROWS, slots), F32)
    for k in range(ids_ref.shape[1]):
        hit = ids_ref[:, k : k + 1] == expert
        chosen = jnp.where(hit, 1.0, chosen)
        weight = jnp.where(hit, gates_ref[:, k : k + 1], weight)
    rank = jnp.zeros((ROWS, slots), F32)
    for t in range(ROWS - 1):
        rank = rank + jnp.where(token > t, chosen[t : t + 1, :], 0.0)
    live = jnp.where(rank == (place % CAPACITY).astype(F32), chosen, 0.0)
    picker = jnp.concatenate([jnp.where(quarter == q, live, 0.0) for q in range(4)], axis=0)
    mixing = jnp.concatenate(
        [jnp.where(quarter == q, live * weight, 0.0) for q in range(4)], axis=0
    )
    return picker, mixing


def layer_kernel(
    chips,
    hidden_ref,
    query_ref,
    keys_ref,
    values_ref,
    new_key_ref,
    new_value_ref,
    gain_ref,
    ids_ref,
    gates_ref,
    gate_hbm,
    up_hbm,
    down_hbm,
    out_ref,
    gate,
    up,
    down,
    outgoing,
    arrived,
    row_buffer,
    gated,
    raised,
    activated,
    mine,
    give,
    take,
    replies,
    answers,
    mixed,
    weight_sem,
    send_sem,
    recv_sem,
    pass_send,
    pass_recv,
    swap_send,
    swap_recv,
    reply_send,
    reply_recv,
):
    width = hidden_ref.shape[1]
    part = width // PARTS
    quarter = part // 4
    plane_rows = chips * CAPACITY
    me = lax.axis_index("ep")
    my_chip, core = me // 2, me % 2
    sibling = my_chip * 2 + (1 - core)

    weight_copies = [
        pltpu.make_async_copy(source.at[0], target, weight_sem.at[i])
        for i, (source, target) in enumerate(((gate_hbm, gate), (up_hbm, up), (down_hbm, down)))
    ]
    for copy in weight_copies:
        copy.start()

    def peer(offset):
        return {"ep": ((my_chip + offset) % chips) * 2 + core}

    barrier = pltpu.get_barrier_semaphore()

    def greet(k, carry):
        pl.semaphore_signal(barrier, inc=1, device_id=peer(k), device_id_type=pl.DeviceIdType.MESH)
        return carry

    lax.fori_loop(1, chips, greet, 0)
    pl.semaphore_signal(
        barrier, inc=1, device_id={"ep": sibling}, device_id_type=pl.DeviceIdType.MESH
    )

    normed = attention_rows(
        hidden_ref, query_ref, keys_ref, values_ref, new_key_ref, new_value_ref, gain_ref
    )
    picker, mixing = slot_weights(ids_ref, gates_ref, chips, my_chip)
    picker = picker.T.astype(BF16)
    mixed[...] = mixing

    def block(k):
        return pl.ds(pl.multiple_of(k * BLOCK, BLOCK), BLOCK)

    def dispatch(h, k):
        return pltpu.make_async_remote_copy(
            src_ref=outgoing.at[h, block(k)],
            dst_ref=arrived.at[h, 0, block(k)],
            send_sem=send_sem.at[h, k],
            recv_sem=recv_sem.at[h, k],
            device_id=peer(k),
            device_id_type=pl.DeviceIdType.MESH,
        )

    def pass_on(h, k):
        return pltpu.make_async_remote_copy(
            src_ref=arrived.at[h, 0, block(k)],
            dst_ref=arrived.at[h, 1, block(k)],
            send_sem=pass_send.at[h, k],
            recv_sem=pass_recv.at[h, k],
            device_id={"ep": sibling},
            device_id_type=pl.DeviceIdType.MESH,
        )

    def swap(h):
        return pltpu.make_async_remote_copy(
            src_ref=give.at[h],
            dst_ref=take.at[h],
            send_sem=swap_send.at[h],
            recv_sem=swap_recv.at[h],
            device_id={"ep": sibling},
            device_id_type=pl.DeviceIdType.MESH,
        )

    def reply(h, k):
        return pltpu.make_async_remote_copy(
            src_ref=replies.at[h, block(k)],
            dst_ref=answers.at[h, block(k)],
            send_sem=reply_send.at[h, k],
            recv_sem=reply_recv.at[h, k],
            device_id=peer(chips - k),
            device_id_type=pl.DeviceIdType.MESH,
        )

    def each(first, body):
        def step(k, carry):
            body(k)
            return carry

        lax.fori_loop(first, chips, step, 0)

    for h in range(PARTS):
        stacked = jnp.concatenate(
            [normed[:, h * part + q * quarter : h * part + (q + 1) * quarter] for q in range(4)],
            axis=0,
        ).astype(BF16)
        packed = jnp.dot(picker, stacked, preferred_element_type=F32).astype(BF16)
        outgoing[h] = packed
        arrived[h, 0, 0:BLOCK] = packed[0:BLOCK]
        if h == 0:
            pl.semaphore_wait(barrier, chips)
        each(1, lambda k: dispatch(h, k).start())
        pass_on(h, 0).start()

    low = lax.broadcasted_iota(jnp.int32, (chips // 2, 8, quarter), 1) < 4

    def swap_halves(x):
        return pltpu.roll(x, 4, axis=1)

    for h in range(PARTS):

        def relay(k):
            dispatch(h, k).wait_recv()
            pass_on(h, k).start()

        each(1, relay)
        for plane in range(2):
            if plane == 1:
                each(0, lambda k: pass_on(h, k).wait_recv())
            tiles = arrived[h, plane].astype(F32).reshape(chips // 2, 2, 2, 8, quarter)
            for p in range(2):
                a, b = tiles[:, 0, p], tiles[:, 1, p]
                first = jnp.where(low, a, b)
                second = swap_halves(jnp.where(low, b, a))
                for q, x in ((2 * p, first), (2 * p + 1, second)):
                    row_buffer[
                        plane * plane_rows : (plane + 1) * plane_rows,
                        h * part + q * quarter : h * part + (q + 1) * quarter,
                    ] = x.reshape(plane_rows, quarter).astype(BF16)
        if h == 0:
            weight_copies[0].wait()
            weight_copies[1].wait()
        x = row_buffer[:, h * part : (h + 1) * part]
        gate_part = jnp.dot(x, gate[h * part : (h + 1) * part, :], preferred_element_type=F32)
        up_part = jnp.dot(x, up[h * part : (h + 1) * part, :], preferred_element_type=F32)
        if h == 0:
            gated[...] = gate_part
            raised[...] = up_part
        else:
            gated[...] += gate_part
            raised[...] += up_part

    activated[...] = (jax.nn.silu(gated[...]) * raised[...]).astype(BF16)
    weight_copies[2].wait()
    for h in range(PARTS):
        for q in range(4):
            columns = slice(h * part + q * quarter, h * part + (q + 1) * quarter)
            y = jnp.dot(activated[...], down[:, columns], preferred_element_type=F32)
            mine[:, columns] = y[:plane_rows]
            give[h, :, q * quarter : (q + 1) * quarter] = y[plane_rows:].astype(BF16)
        swap(h).start()
    for h in range(PARTS):
        swap(h).wait_recv()
        halves = []
        for p in range(2):
            y = []
            for q in (2 * p, 2 * p + 1):
                columns = slice(h * part + q * quarter, h * part + (q + 1) * quarter)
                whole = mine[:, columns] + take[h, :, q * quarter : (q + 1) * quarter].astype(F32)
                y.append(whole.reshape(chips // 2, 8, quarter))
            turned = swap_halves(y[1])
            halves.append((jnp.where(low, y[0], turned), jnp.where(low, turned, y[0])))
        for m in range(chips // 2):
            for side in range(2):
                start = (2 * m + side) * BLOCK
                replies[h, start : start + BLOCK] = jnp.concatenate(
                    [halves[0][side][m], halves[1][side][m]], axis=0
                ).astype(BF16)
        answers[h, 0:BLOCK] = replies[h, 0:BLOCK]
        each(1, lambda k: reply(h, k).start())

    mixing = mixed[...]
    high = mixing.astype(BF16)
    rest = mixing - high.astype(F32)
    middle = rest.astype(BF16)
    last = (rest - middle.astype(F32)).astype(BF16)
    for h in range(PARTS):
        each(1, lambda k: reply(h, k).wait_recv())
        got = answers[h]
        total = jnp.dot(high, got, preferred_element_type=F32)
        total = total + jnp.dot(middle, got, preferred_element_type=F32)
        total = total + jnp.dot(last, got, preferred_element_type=F32)
        for q in range(4):
            columns = slice(h * part + q * quarter, h * part + (q + 1) * quarter)
            out_ref[:, columns] = total[q * ROWS : (q + 1) * ROWS].astype(out_ref.dtype)

    for h in range(PARTS):
        each(1, lambda k: dispatch(h, k).wait_send())
        each(0, lambda k: pass_on(h, k).wait_send())
        swap(h).wait_send()
        each(1, lambda k: reply(h, k).wait_send())


def fused_layer(
    hidden,
    query,
    cached_key_store,
    cached_value_store,
    current_key,
    current_value,
    norm_gain,
    expert_ids,
    gate_weights,
    w_gate,
    w_up,
    w_down,
):
    chips = lax.axis_size("ep") // 2
    width = hidden.shape[1]
    part = width // PARTS
    slots = chips * BLOCK
    units = w_gate.shape[2]
    pair_rows = 2 * chips * CAPACITY
    dma = pltpu.SemaphoreType.DMA
    vmem = pl.BlockSpec(memory_space=pltpu.VMEM)
    hbm = pl.BlockSpec(memory_space=pl.ANY)
    return pl.pallas_call(
        functools.partial(layer_kernel, chips),
        out_shape=jax.ShapeDtypeStruct(hidden.shape, BF16),
        in_specs=[vmem] * 9 + [hbm] * 3,
        out_specs=vmem,
        scratch_shapes=[
            pltpu.VMEM((width, units), BF16),
            pltpu.VMEM((width, units), BF16),
            pltpu.VMEM((units, width), BF16),
            pltpu.VMEM((PARTS, slots, part // 4), BF16),
            pltpu.VMEM((PARTS, 2, slots, part // 4), BF16),
            pltpu.VMEM((pair_rows, width), BF16),
            pltpu.VMEM((pair_rows, units), F32),
            pltpu.VMEM((pair_rows, units), F32),
            pltpu.VMEM((pair_rows, units), BF16),
            pltpu.VMEM((pair_rows // 2, width), F32),
            pltpu.VMEM((PARTS, pair_rows // 2, part), BF16),
            pltpu.VMEM((PARTS, pair_rows // 2, part), BF16),
            pltpu.VMEM((PARTS, slots, part // 4), BF16),
            pltpu.VMEM((PARTS, slots, part // 4), BF16),
            pltpu.VMEM((4 * ROWS, slots), F32),
            dma((3,)),
            dma((PARTS, chips)),
            dma((PARTS, chips)),
            dma((PARTS, chips)),
            dma((PARTS, chips)),
            dma((PARTS,)),
            dma((PARTS,)),
            dma((PARTS, chips)),
            dma((PARTS, chips)),
        ],
        compiler_params=pltpu.CompilerParams(
            collective_id=0, has_side_effects=True, vmem_limit_bytes=48 * 1024 * 1024
        ),
        cost_estimate=pl.CostEstimate(
            flops=6 * pair_rows * width * units,
            bytes_accessed=6 * width * units,
            transcendentals=pair_rows * units,
        ),
    )(
        hidden,
        query,
        cached_key_store,
        cached_value_store,
        current_key,
        current_value,
        norm_gain.reshape(1, width),
        expert_ids,
        gate_weights,
        w_gate,
        w_up,
        w_down,
    )


def takes_fused_layer(row_count, chosen_count, units):
    if lax.axis_size("sub") != 1 or lax.axis_size("group") != 1 or 2 * units != FF:
        return False
    chips = lax.axis_size("ep") // 2
    return row_count == ROWS and chips * CAPACITY == row_count * chosen_count and chips % 2 == 0


def shards(
    hidden,
    query,
    cached_key_store,
    cached_value_store,
    current_key,
    current_value,
    norm_gain,
    expert_ids,
    gate_weights,
    w_gate,
    w_up,
    w_down,
):
    ep_count = lax.axis_size("ep")
    sub_count = lax.axis_size("sub")
    sub_place = lax.axis_index("sub")
    count_of_rows = hidden.shape[0]
    if takes_fused_layer(hidden.shape[0], expert_ids.shape[1], w_gate.shape[2]):
        return fused_layer(
            hidden,
            query,
            cached_key_store,
            cached_value_store,
            current_key,
            current_value,
            norm_gain,
            expert_ids,
            gate_weights,
            w_gate,
            w_up,
            w_down,
        )
    chosen_count = expert_ids.shape[1]
    slice_units = sub_count * w_gate.shape[2]
    spread = FF // slice_units
    experts = ep_count // spread
    capacity = max(2, count_of_rows * chosen_count // experts)
    ids_pair = expert_ids.reshape(sub_count, count_of_rows, chosen_count)
    gates_pair = gate_weights.reshape(sub_count, count_of_rows, chosen_count)
    normed = attend_norm(
        hidden, query, cached_key_store, cached_value_store, current_key, current_value, norm_gain
    )
    merged = moe_block(
        normed, ids_pair, gates_pair, w_gate, w_up, w_down, experts, spread, capacity, sub_place
    )
    return merged.reshape(sub_count * count_of_rows, merged.shape[2])


def solution(mesh):
    return jax.shard_map(
        shards,
        mesh=mesh,
        in_specs=(
            P(("group", "ep", "sub"), None),
            P(("group", "ep", "sub"), None),
            P(("group", "ep", "sub"), None, None),
            P(("group", "ep", "sub"), None, None),
            P(("group", "ep", "sub"), None),
            P(("group", "ep", "sub"), None),
            P(),
            P(("group", "ep"), None),
            P(("group", "ep"), None),
            P("ep", None, "sub"),
            P("ep", None, "sub"),
            P("ep", None, "sub"),
        ),
        out_specs=P(("group", "ep"), "sub"),
        check_vma=False,
    )
```

```python
import functools
import math

import jax
import jax.numpy as jnp
from jax import lax
from jax.experimental import pallas as pl
from jax.experimental.pallas import tpu as pltpu
from jax.sharding import PartitionSpec as P

QUERY_HEADS = 32
KEY_VALUE_HEADS = 2
HEAD_SIZE = 128
FF = 768


epsilon = 1e-06


def attend_norm(
    hidden, query, cached_key_store, cached_value_store, current_key, current_value, norm_gain
):
    count_of_rows = hidden.shape[0]
    context_output = cached_key_store.shape[1]
    query_group_width = QUERY_HEADS // KEY_VALUE_HEADS
    scaling = 1.0 / math.sqrt(HEAD_SIZE)
    query_rows = query.reshape(count_of_rows, KEY_VALUE_HEADS, query_group_width, HEAD_SIZE)
    key_row_block = cached_key_store.reshape(
        count_of_rows, context_output, KEY_VALUE_HEADS, HEAD_SIZE
    )
    value_row_block = cached_value_store.reshape(
        count_of_rows, context_output, KEY_VALUE_HEADS, HEAD_SIZE
    )
    incoming_key = current_key.reshape(count_of_rows, KEY_VALUE_HEADS, HEAD_SIZE)
    incoming_value = current_value.reshape(count_of_rows, KEY_VALUE_HEADS, HEAD_SIZE)
    old_scores = (
        jnp.einsum("tgqd,tpgd->tgqp", query_rows, key_row_block, preferred_element_type=jnp.float32)
        * scaling
    )
    new_scores = (
        jnp.einsum("tgqd,tgd->tgq", query_rows, incoming_key, preferred_element_type=jnp.float32)
        * scaling
    )
    top_score = jnp.maximum(jnp.max(old_scores, axis=-1), new_scores)
    old_exp = jnp.exp(old_scores - top_score[..., None])
    new_exp = jnp.exp(new_scores - top_score)
    denominator = jnp.sum(old_exp, axis=-1) + new_exp
    old_probs = (old_exp / denominator[..., None]).astype(jnp.bfloat16)
    new_probs = (new_exp / denominator).astype(jnp.bfloat16)
    attended = jnp.einsum(
        "tgqp,tpgd->tgqd", old_probs, value_row_block, preferred_element_type=jnp.float32
    )
    attended = (
        attended
        + new_probs.astype(jnp.float32)[..., None]
        * incoming_value.astype(jnp.float32)[:, :, None, :]
    )
    resid = hidden.astype(jnp.float32) + attended.reshape(count_of_rows, QUERY_HEADS * HEAD_SIZE)
    meansq = jnp.mean(resid * resid, axis=-1, keepdims=True)
    return (resid * lax.rsqrt(meansq + epsilon) * norm_gain).astype(jnp.bfloat16)


def slot_targets(chosen, experts, capacity):
    flattened = chosen.reshape(-1)
    onehot = (flattened[:, None] == jnp.arange(experts, dtype=jnp.int32)[None, :]).astype(jnp.int32)
    slot_rank = jnp.sum((jnp.cumsum(onehot, axis=0) - onehot) * onehot, axis=1)
    return (flattened * capacity + slot_rank).reshape(chosen.shape)


def pack_rows(normed, target, experts, capacity, spread):
    model_width = normed.shape[1]
    all_slots = jnp.arange(experts * capacity, dtype=jnp.int32)
    match = all_slots[:, None, None] == target[None, :, :]
    picker = jnp.any(match, axis=2).astype(jnp.bfloat16)
    packed = jnp.dot(picker, normed, preferred_element_type=jnp.float32).astype(jnp.bfloat16)
    packed = packed.reshape(experts, 1, capacity, model_width)
    widened = jnp.broadcast_to(packed, (experts, spread, capacity, model_width))
    return widened.reshape(experts * spread, capacity, model_width)


def expert_hidden(slot_rows, w_gate, w_up):
    flattened = slot_rows.reshape(-1, slot_rows.shape[-1])
    gated = jnp.dot(flattened, w_gate[0], preferred_element_type=jnp.float32)
    raised = jnp.dot(flattened, w_up[0], preferred_element_type=jnp.float32)
    activated = (jax.nn.silu(gated) * raised).astype(jnp.bfloat16)
    return activated.reshape(slot_rows.shape[:-1] + (activated.shape[1],))


def expert_down(activated, w_down):
    out_width = w_down.shape[2]
    portion = lax.all_gather(activated, "sub", axis=3, tiled=True)
    unit_rows = portion.reshape(-1, portion.shape[-1])
    unit_weights = w_down[0]
    running = jnp.dot(unit_rows, unit_weights, preferred_element_type=jnp.float32)
    return running.astype(jnp.bfloat16).reshape(activated.shape[:3] + (out_width,))


def moe_block(
    normed, ids_pair, gates_pair, w_gate, w_up, w_down, experts, spread, capacity, sub_place
):
    pair_count = ids_pair.shape[0]
    count_of_rows = ids_pair.shape[1]
    targets = jnp.stack(
        [slot_targets(ids_pair[side], experts, capacity) for side in range(pair_count)]
    )
    own_targets = lax.dynamic_index_in_dim(targets, sub_place, 0, keepdims=False)
    outgoing = pack_rows(normed, own_targets, experts, capacity, spread)
    arrived = lax.all_to_all(outgoing, "ep", split_axis=0, concat_axis=0, tiled=True)
    activated = expert_hidden(
        lax.all_gather(arrived[None], "sub", axis=0, tiled=True), w_gate, w_up
    )
    partial_rows = expert_down(activated, w_down)
    returned = lax.all_to_all(partial_rows, "ep", split_axis=1, concat_axis=1, tiled=True)
    shaped = returned.reshape(pair_count, experts, spread, capacity, returned.shape[3])
    summed = jnp.sum(shaped, axis=2, dtype=jnp.float32)
    contract = "snec,sech->snh"
    columns = jnp.arange(experts * capacity, dtype=jnp.int32)
    selected = (targets[..., None] == columns).astype(jnp.float32)
    mixing = jnp.einsum("snk,snkc->snc", gates_pair, selected, precision=lax.Precision.HIGHEST)
    mixing = mixing.reshape(pair_count, count_of_rows, experts, capacity)
    return jnp.einsum(contract, mixing, summed, precision=lax.Precision.HIGHEST).astype(
        jnp.bfloat16
    )


CAPACITY = 4
ROWS = 8
BLOCK = 16
PARTS = 2
F32 = jnp.float32
BF16 = jnp.bfloat16


def attention_rows(hidden_ref, query_ref, keys_ref, values_ref, new_key_ref, new_value_ref, gain_ref):
    positions = keys_ref.shape[1]
    group = QUERY_HEADS // KEY_VALUE_HEADS
    scaling = 1.0 / math.sqrt(HEAD_SIZE)
    query = query_ref[...].astype(F32)
    rows, columns = group * ROWS, ROWS * positions
    row_token = lax.broadcasted_iota(jnp.int32, (rows, columns), 0) % ROWS
    column_token = lax.broadcasted_iota(jnp.int32, (rows, columns), 1) // positions
    own = row_token == column_token
    pieces = []
    for g in range(KEY_VALUE_HEADS):
        lanes = slice(g * HEAD_SIZE, (g + 1) * HEAD_SIZE)
        stacked = jnp.concatenate(
            [
                query[:, (g * group + h) * HEAD_SIZE : (g * group + h + 1) * HEAD_SIZE]
                for h in range(group)
            ],
            axis=0,
        )
        keys = keys_ref[:, :, lanes].reshape(columns, HEAD_SIZE)
        values = values_ref[:, :, lanes].reshape(columns, HEAD_SIZE)
        scores = lax.dot_general(
            stacked.astype(BF16), keys, (((1,), (1,)), ((), ())), preferred_element_type=F32
        )
        scores = jnp.where(own, scores * scaling, -1e30)
        new_key = jnp.concatenate([new_key_ref[:, lanes].astype(F32)] * group, axis=0)
        new_value = jnp.concatenate([new_value_ref[:, lanes].astype(F32)] * group, axis=0)
        new_score = jnp.sum(stacked * new_key, axis=1, keepdims=True) * scaling
        top = jnp.maximum(jnp.max(scores, axis=1, keepdims=True), new_score)
        weights = jnp.exp(scores - top)
        new_weight = jnp.exp(new_score - top)
        total = jnp.sum(weights, axis=1, keepdims=True) + new_weight
        probs = (weights / total).astype(BF16)
        new_prob = (new_weight / total).astype(BF16).astype(F32)
        attended = jnp.dot(probs, values, preferred_element_type=F32) + new_prob * new_value
        pieces += [attended[h * ROWS : (h + 1) * ROWS] for h in range(group)]
    resid = hidden_ref[...].astype(F32) + jnp.concatenate(pieces, axis=1)
    meansq = jnp.mean(resid * resid, axis=1, keepdims=True)
    return resid * lax.rsqrt(meansq + epsilon) * gain_ref[...]


def slot_weights(ids_ref, gates_ref, chips, my_chip):
    slots = chips * BLOCK
    place = lax.broadcasted_iota(jnp.int32, (ROWS, slots), 1)
    token = lax.broadcasted_iota(jnp.int32, (ROWS, slots), 0)
    expert = (place // BLOCK + my_chip) % chips
    quarter = 2 * ((place // 8) % 2) + ((place // 4) % 2 + (place // BLOCK) % 2) % 2
    chosen = jnp.zeros((ROWS, slots), F32)
    weight = jnp.zeros((ROWS, slots), F32)
    for k in range(ids_ref.shape[1]):
        hit = ids_ref[:, k : k + 1] == expert
        chosen = jnp.where(hit, 1.0, chosen)
        weight = jnp.where(hit, gates_ref[:, k : k + 1], weight)
    rank = jnp.zeros((ROWS, slots), F32)
    for t in range(ROWS - 1):
        rank = rank + jnp.where(token > t, chosen[t : t + 1, :], 0.0)
    live = jnp.where(rank == (place % CAPACITY).astype(F32), chosen, 0.0)
    picker = jnp.concatenate([jnp.where(quarter == q, live, 0.0) for q in range(4)], axis=0)
    mixing = jnp.concatenate(
        [jnp.where(quarter == q, live * weight, 0.0) for q in range(4)], axis=0
    )
    return picker, mixing


def layer_kernel(
    chips,
    hidden_hbm,
    query_hbm,
    keys_hbm,
    values_hbm,
    new_key_hbm,
    new_value_hbm,
    gain_hbm,
    ids_hbm,
    gates_hbm,
    gate_hbm,
    up_hbm,
    down_hbm,
    out_ref,
    hidden_ref,
    query_ref,
    keys_ref,
    values_ref,
    new_key_ref,
    new_value_ref,
    gain_ref,
    ids_ref,
    gates_ref,
    gate,
    up,
    down,
    outgoing,
    arrived,
    row_buffer,
    gated,
    raised,
    activated,
    mine,
    give,
    take,
    replies,
    answers,
    mixed,
    input_sem,
    weight_sem,
    send_sem,
    recv_sem,
    pass_send,
    pass_recv,
    swap_send,
    swap_recv,
    reply_send,
    reply_recv,
):
    width = hidden_ref.shape[1]
    part = width // PARTS
    quarter = part // 4
    plane_rows = chips * CAPACITY
    me = lax.axis_index("ep")
    my_chip, core = me // 2, me % 2
    sibling = my_chip * 2 + (1 - core)

    staged = (
        (query_hbm, query_ref),
        (keys_hbm, keys_ref),
        (values_hbm, values_ref),
        (new_key_hbm, new_key_ref),
        (new_value_hbm, new_value_ref),
        (hidden_hbm, hidden_ref),
        (gain_hbm, gain_ref),
        (ids_hbm, ids_ref),
        (gates_hbm, gates_ref),
    )
    input_copies = [
        pltpu.make_async_copy(source, target, input_sem.at[i])
        for i, (source, target) in enumerate(staged)
    ]
    for copy in input_copies:
        copy.start()
    weight_copies = [
        pltpu.make_async_copy(source.at[0], target, weight_sem.at[i])
        for i, (source, target) in enumerate(((gate_hbm, gate), (up_hbm, up), (down_hbm, down)))
    ]
    for copy in weight_copies:
        copy.start()

    def peer(offset):
        return {"ep": ((my_chip + offset) % chips) * 2 + core}

    barrier = pltpu.get_barrier_semaphore()

    def greet(k, carry):
        pl.semaphore_signal(barrier, inc=1, device_id=peer(k), device_id_type=pl.DeviceIdType.MESH)
        return carry

    lax.fori_loop(1, chips, greet, 0)
    pl.semaphore_signal(
        barrier, inc=1, device_id={"ep": sibling}, device_id_type=pl.DeviceIdType.MESH
    )

    for copy in input_copies:
        copy.wait()
    normed = attention_rows(
        hidden_ref, query_ref, keys_ref, values_ref, new_key_ref, new_value_ref, gain_ref
    )
    picker, mixing = slot_weights(ids_ref, gates_ref, chips, my_chip)
    picker = picker.T.astype(BF16)
    mixed[...] = mixing

    def block(k):
        return pl.ds(pl.multiple_of(k * BLOCK, BLOCK), BLOCK)

    def dispatch(h, k):
        return pltpu.make_async_remote_copy(
            src_ref=outgoing.at[h, block(k)],
            dst_ref=arrived.at[h, 0, block(k)],
            send_sem=send_sem.at[h, k],
            recv_sem=recv_sem.at[h, k],
            device_id=peer(k),
            device_id_type=pl.DeviceIdType.MESH,
        )

    def pass_on(h, k):
        return pltpu.make_async_remote_copy(
            src_ref=arrived.at[h, 0, block(k)],
            dst_ref=arrived.at[h, 1, block(k)],
            send_sem=pass_send.at[h, k],
            recv_sem=pass_recv.at[h, k],
            device_id={"ep": sibling},
            device_id_type=pl.DeviceIdType.MESH,
        )

    def swap(h):
        return pltpu.make_async_remote_copy(
            src_ref=give.at[h],
            dst_ref=take.at[h],
            send_sem=swap_send.at[h],
            recv_sem=swap_recv.at[h],
            device_id={"ep": sibling},
            device_id_type=pl.DeviceIdType.MESH,
        )

    def reply(h, k):
        return pltpu.make_async_remote_copy(
            src_ref=replies.at[h, block(k)],
            dst_ref=answers.at[h, block(k)],
            send_sem=reply_send.at[h, k],
            recv_sem=reply_recv.at[h, k],
            device_id=peer(chips - k),
            device_id_type=pl.DeviceIdType.MESH,
        )

    def each(first, body):
        def step(k, carry):
            body(k)
            return carry

        lax.fori_loop(first, chips, step, 0)

    for h in range(PARTS):
        stacked = jnp.concatenate(
            [normed[:, h * part + q * quarter : h * part + (q + 1) * quarter] for q in range(4)],
            axis=0,
        ).astype(BF16)
        packed = jnp.dot(picker, stacked, preferred_element_type=F32).astype(BF16)
        outgoing[h] = packed
        arrived[h, 0, 0:BLOCK] = packed[0:BLOCK]
        if h == 0:
            pl.semaphore_wait(barrier, chips)
        each(1, lambda k: dispatch(h, k).start())
        pass_on(h, 0).start()

    low = lax.broadcasted_iota(jnp.int32, (chips // 2, 8, quarter), 1) < 4

    def swap_halves(x):
        return pltpu.roll(x, 4, axis=1)

    for h in range(PARTS):

        def relay(k):
            dispatch(h, k).wait_recv()
            pass_on(h, k).start()

        each(1, relay)
        for plane in range(2):
            if plane == 1:
                each(0, lambda k: pass_on(h, k).wait_recv())
            tiles = arrived[h, plane].astype(F32).reshape(chips // 2, 2, 2, 8, quarter)
            for p in range(2):
                a, b = tiles[:, 0, p], tiles[:, 1, p]
                first = jnp.where(low, a, b)
                second = swap_halves(jnp.where(low, b, a))
                for q, x in ((2 * p, first), (2 * p + 1, second)):
                    row_buffer[
                        plane * plane_rows : (plane + 1) * plane_rows,
                        h * part + q * quarter : h * part + (q + 1) * quarter,
                    ] = x.reshape(plane_rows, quarter).astype(BF16)
        if h == 0:
            weight_copies[0].wait()
            weight_copies[1].wait()
        x = row_buffer[:, h * part : (h + 1) * part]
        gate_part = jnp.dot(x, gate[h * part : (h + 1) * part, :], preferred_element_type=F32)
        up_part = jnp.dot(x, up[h * part : (h + 1) * part, :], preferred_element_type=F32)
        if h == 0:
            gated[...] = gate_part
            raised[...] = up_part
        else:
            gated[...] += gate_part
            raised[...] += up_part

    activated[...] = (jax.nn.silu(gated[...]) * raised[...]).astype(BF16)
    weight_copies[2].wait()
    for h in range(PARTS):
        for q in range(4):
            columns = slice(h * part + q * quarter, h * part + (q + 1) * quarter)
            y = jnp.dot(activated[...], down[:, columns], preferred_element_type=F32)
            mine[:, columns] = y[:plane_rows]
            give[h, :, q * quarter : (q + 1) * quarter] = y[plane_rows:].astype(BF16)
        swap(h).start()
    for h in range(PARTS):
        swap(h).wait_recv()
        halves = []
        for p in range(2):
            y = []
            for q in (2 * p, 2 * p + 1):
                columns = slice(h * part + q * quarter, h * part + (q + 1) * quarter)
                whole = mine[:, columns] + take[h, :, q * quarter : (q + 1) * quarter].astype(F32)
                y.append(whole.reshape(chips // 2, 8, quarter))
            turned = swap_halves(y[1])
            halves.append((jnp.where(low, y[0], turned), jnp.where(low, turned, y[0])))
        for m in range(chips // 2):
            for side in range(2):
                start = (2 * m + side) * BLOCK
                replies[h, start : start + BLOCK] = jnp.concatenate(
                    [halves[0][side][m], halves[1][side][m]], axis=0
                ).astype(BF16)
        answers[h, 0:BLOCK] = replies[h, 0:BLOCK]
        each(1, lambda k: reply(h, k).start())

    mixing = mixed[...]
    high = mixing.astype(BF16)
    rest = mixing - high.astype(F32)
    middle = rest.astype(BF16)
    last = (rest - middle.astype(F32)).astype(BF16)
    for h in range(PARTS):
        each(1, lambda k: reply(h, k).wait_recv())
        got = answers[h]
        total = jnp.dot(high, got, preferred_element_type=F32)
        total = total + jnp.dot(middle, got, preferred_element_type=F32)
        total = total + jnp.dot(last, got, preferred_element_type=F32)
        for q in range(4):
            columns = slice(h * part + q * quarter, h * part + (q + 1) * quarter)
            out_ref[:, columns] = total[q * ROWS : (q + 1) * ROWS].astype(out_ref.dtype)

    for h in range(PARTS):
        each(1, lambda k: dispatch(h, k).wait_send())
        each(0, lambda k: pass_on(h, k).wait_send())
        swap(h).wait_send()
        each(1, lambda k: reply(h, k).wait_send())


def fused_layer(
    hidden,
    query,
    cached_key_store,
    cached_value_store,
    current_key,
    current_value,
    norm_gain,
    expert_ids,
    gate_weights,
    w_gate,
    w_up,
    w_down,
):
    chips = lax.axis_size("ep") // 2
    width = hidden.shape[1]
    part = width // PARTS
    slots = chips * BLOCK
    units = w_gate.shape[2]
    pair_rows = 2 * chips * CAPACITY
    small = (
        hidden,
        query,
        cached_key_store,
        cached_value_store,
        current_key,
        current_value,
        norm_gain.reshape(1, width),
        expert_ids,
        gate_weights,
    )
    dma = pltpu.SemaphoreType.DMA
    vmem = pl.BlockSpec(memory_space=pltpu.VMEM)
    hbm = pl.BlockSpec(memory_space=pltpu.HBM)
    return pl.pallas_call(
        functools.partial(layer_kernel, chips),
        out_shape=jax.ShapeDtypeStruct(hidden.shape, BF16),
        in_specs=[hbm] * 12,
        out_specs=vmem,
        scratch_shapes=[pltpu.VMEM(x.shape, x.dtype) for x in small]
        + [
            pltpu.VMEM((width, units), BF16),
            pltpu.VMEM((width, units), BF16),
            pltpu.VMEM((units, width), BF16),
            pltpu.VMEM((PARTS, slots, part // 4), BF16),
            pltpu.VMEM((PARTS, 2, slots, part // 4), BF16),
            pltpu.VMEM((pair_rows, width), BF16),
            pltpu.VMEM((pair_rows, units), F32),
            pltpu.VMEM((pair_rows, units), F32),
            pltpu.VMEM((pair_rows, units), BF16),
            pltpu.VMEM((pair_rows // 2, width), F32),
            pltpu.VMEM((PARTS, pair_rows // 2, part), BF16),
            pltpu.VMEM((PARTS, pair_rows // 2, part), BF16),
            pltpu.VMEM((PARTS, slots, part // 4), BF16),
            pltpu.VMEM((PARTS, slots, part // 4), BF16),
            pltpu.VMEM((4 * ROWS, slots), F32),
            dma((9,)),
            dma((3,)),
            dma((PARTS, chips)),
            dma((PARTS, chips)),
            dma((PARTS, chips)),
            dma((PARTS, chips)),
            dma((PARTS,)),
            dma((PARTS,)),
            dma((PARTS, chips)),
            dma((PARTS, chips)),
        ],
        compiler_params=pltpu.CompilerParams(
            collective_id=0, has_side_effects=True, vmem_limit_bytes=62 * 1024 * 1024
        ),
        cost_estimate=pl.CostEstimate(
            flops=6 * pair_rows * width * units,
            bytes_accessed=6 * width * units,
            transcendentals=pair_rows * units,
        ),
    )(*small, w_gate, w_up, w_down)


def takes_fused_layer(row_count, chosen_count, units):
    if lax.axis_size("sub") != 1 or lax.axis_size("group") != 1 or 2 * units != FF:
        return False
    chips = lax.axis_size("ep") // 2
    return row_count == ROWS and chips * CAPACITY == row_count * chosen_count and chips % 2 == 0


def shards(
    hidden,
    query,
    cached_key_store,
    cached_value_store,
    current_key,
    current_value,
    norm_gain,
    expert_ids,
    gate_weights,
    w_gate,
    w_up,
    w_down,
):
    ep_count = lax.axis_size("ep")
    sub_count = lax.axis_size("sub")
    sub_place = lax.axis_index("sub")
    count_of_rows = hidden.shape[0]
    if takes_fused_layer(hidden.shape[0], expert_ids.shape[1], w_gate.shape[2]):
        return fused_layer(
            hidden,
            query,
            cached_key_store,
            cached_value_store,
            current_key,
            current_value,
            norm_gain,
            expert_ids,
            gate_weights,
            w_gate,
            w_up,
            w_down,
        )
    chosen_count = expert_ids.shape[1]
    slice_units = sub_count * w_gate.shape[2]
    spread = FF // slice_units
    experts = ep_count // spread
    capacity = max(2, count_of_rows * chosen_count // experts)
    ids_pair = expert_ids.reshape(sub_count, count_of_rows, chosen_count)
    gates_pair = gate_weights.reshape(sub_count, count_of_rows, chosen_count)
    normed = attend_norm(
        hidden, query, cached_key_store, cached_value_store, current_key, current_value, norm_gain
    )
    merged = moe_block(
        normed, ids_pair, gates_pair, w_gate, w_up, w_down, experts, spread, capacity, sub_place
    )
    return merged.reshape(sub_count * count_of_rows, merged.shape[2])


def solution(mesh):
    return jax.shard_map(
        shards,
        mesh=mesh,
        in_specs=(
            P(("group", "ep", "sub"), None),
            P(("group", "ep", "sub"), None),
            P(("group", "ep", "sub"), None, None),
            P(("group", "ep", "sub"), None, None),
            P(("group", "ep", "sub"), None),
            P(("group", "ep", "sub"), None),
            P(),
            P(("group", "ep"), None),
            P(("group", "ep"), None),
            P("ep", None, "sub"),
            P("ep", None, "sub"),
            P("ep", None, "sub"),
        ),
        out_specs=P(("group", "ep"), "sub"),
        check_vma=False,
    )
```

```python
import functools
import math

import jax
import jax.numpy as jnp
from jax import lax
from jax.experimental import pallas as pl
from jax.experimental.pallas import tpu as pltpu
from jax.sharding import PartitionSpec as P

QUERY_HEADS = 32
KEY_VALUE_HEADS = 2
HEAD_SIZE = 128
FF = 768


epsilon = 1e-06


def attend_norm(
    hidden, query, cached_key_store, cached_value_store, current_key, current_value, norm_gain
):
    count_of_rows = hidden.shape[0]
    context_output = cached_key_store.shape[1]
    query_group_width = QUERY_HEADS // KEY_VALUE_HEADS
    scaling = 1.0 / math.sqrt(HEAD_SIZE)
    query_rows = query.reshape(count_of_rows, KEY_VALUE_HEADS, query_group_width, HEAD_SIZE)
    key_row_block = cached_key_store.reshape(
        count_of_rows, context_output, KEY_VALUE_HEADS, HEAD_SIZE
    )
    value_row_block = cached_value_store.reshape(
        count_of_rows, context_output, KEY_VALUE_HEADS, HEAD_SIZE
    )
    incoming_key = current_key.reshape(count_of_rows, KEY_VALUE_HEADS, HEAD_SIZE)
    incoming_value = current_value.reshape(count_of_rows, KEY_VALUE_HEADS, HEAD_SIZE)
    old_scores = (
        jnp.einsum("tgqd,tpgd->tgqp", query_rows, key_row_block, preferred_element_type=jnp.float32)
        * scaling
    )
    new_scores = (
        jnp.einsum("tgqd,tgd->tgq", query_rows, incoming_key, preferred_element_type=jnp.float32)
        * scaling
    )
    top_score = jnp.maximum(jnp.max(old_scores, axis=-1), new_scores)
    old_exp = jnp.exp(old_scores - top_score[..., None])
    new_exp = jnp.exp(new_scores - top_score)
    denominator = jnp.sum(old_exp, axis=-1) + new_exp
    old_probs = (old_exp / denominator[..., None]).astype(jnp.bfloat16)
    new_probs = (new_exp / denominator).astype(jnp.bfloat16)
    attended = jnp.einsum(
        "tgqp,tpgd->tgqd", old_probs, value_row_block, preferred_element_type=jnp.float32
    )
    attended = (
        attended
        + new_probs.astype(jnp.float32)[..., None]
        * incoming_value.astype(jnp.float32)[:, :, None, :]
    )
    resid = hidden.astype(jnp.float32) + attended.reshape(count_of_rows, QUERY_HEADS * HEAD_SIZE)
    meansq = jnp.mean(resid * resid, axis=-1, keepdims=True)
    return (resid * lax.rsqrt(meansq + epsilon) * norm_gain).astype(jnp.bfloat16)


def slot_targets(chosen, experts, capacity):
    flattened = chosen.reshape(-1)
    onehot = (flattened[:, None] == jnp.arange(experts, dtype=jnp.int32)[None, :]).astype(jnp.int32)
    slot_rank = jnp.sum((jnp.cumsum(onehot, axis=0) - onehot) * onehot, axis=1)
    return (flattened * capacity + slot_rank).reshape(chosen.shape)


def pack_rows(normed, target, experts, capacity, spread):
    model_width = normed.shape[1]
    all_slots = jnp.arange(experts * capacity, dtype=jnp.int32)
    match = all_slots[:, None, None] == target[None, :, :]
    picker = jnp.any(match, axis=2).astype(jnp.bfloat16)
    packed = jnp.dot(picker, normed, preferred_element_type=jnp.float32).astype(jnp.bfloat16)
    packed = packed.reshape(experts, 1, capacity, model_width)
    widened = jnp.broadcast_to(packed, (experts, spread, capacity, model_width))
    return widened.reshape(experts * spread, capacity, model_width)


def expert_hidden(slot_rows, w_gate, w_up):
    flattened = slot_rows.reshape(-1, slot_rows.shape[-1])
    gated = jnp.dot(flattened, w_gate[0], preferred_element_type=jnp.float32)
    raised = jnp.dot(flattened, w_up[0], preferred_element_type=jnp.float32)
    activated = (jax.nn.silu(gated) * raised).astype(jnp.bfloat16)
    return activated.reshape(slot_rows.shape[:-1] + (activated.shape[1],))


def expert_down(activated, w_down):
    out_width = w_down.shape[2]
    portion = lax.all_gather(activated, "sub", axis=3, tiled=True)
    unit_rows = portion.reshape(-1, portion.shape[-1])
    unit_weights = w_down[0]
    running = jnp.dot(unit_rows, unit_weights, preferred_element_type=jnp.float32)
    return running.astype(jnp.bfloat16).reshape(activated.shape[:3] + (out_width,))


def moe_block(
    normed, ids_pair, gates_pair, w_gate, w_up, w_down, experts, spread, capacity, sub_place
):
    pair_count = ids_pair.shape[0]
    count_of_rows = ids_pair.shape[1]
    targets = jnp.stack(
        [slot_targets(ids_pair[side], experts, capacity) for side in range(pair_count)]
    )
    own_targets = lax.dynamic_index_in_dim(targets, sub_place, 0, keepdims=False)
    outgoing = pack_rows(normed, own_targets, experts, capacity, spread)
    arrived = lax.all_to_all(outgoing, "ep", split_axis=0, concat_axis=0, tiled=True)
    activated = expert_hidden(
        lax.all_gather(arrived[None], "sub", axis=0, tiled=True), w_gate, w_up
    )
    partial_rows = expert_down(activated, w_down)
    returned = lax.all_to_all(partial_rows, "ep", split_axis=1, concat_axis=1, tiled=True)
    shaped = returned.reshape(pair_count, experts, spread, capacity, returned.shape[3])
    summed = jnp.sum(shaped, axis=2, dtype=jnp.float32)
    contract = "snec,sech->snh"
    columns = jnp.arange(experts * capacity, dtype=jnp.int32)
    selected = (targets[..., None] == columns).astype(jnp.float32)
    mixing = jnp.einsum("snk,snkc->snc", gates_pair, selected, precision=lax.Precision.HIGHEST)
    mixing = mixing.reshape(pair_count, count_of_rows, experts, capacity)
    return jnp.einsum(contract, mixing, summed, precision=lax.Precision.HIGHEST).astype(
        jnp.bfloat16
    )


CAPACITY = 4
ROWS = 8
BLOCK = 16
PARTS = 2
PLANE = 4
F32 = jnp.float32
BF16 = jnp.bfloat16


def attention_rows(hidden_ref, query_ref, keys_ref, values_ref, new_key_ref, new_value_ref, gain_ref):
    positions = keys_ref.shape[1]
    group = QUERY_HEADS // KEY_VALUE_HEADS
    scaling = 1.0 / math.sqrt(HEAD_SIZE)
    query = query_ref[...].astype(F32)
    rows, columns = group * ROWS, ROWS * positions
    row_token = lax.broadcasted_iota(jnp.int32, (rows, columns), 0) % ROWS
    column_token = lax.broadcasted_iota(jnp.int32, (rows, columns), 1) // positions
    own = row_token == column_token
    pieces = []
    for g in range(KEY_VALUE_HEADS):
        lanes = slice(g * HEAD_SIZE, (g + 1) * HEAD_SIZE)
        stacked = jnp.concatenate(
            [
                query[:, (g * group + h) * HEAD_SIZE : (g * group + h + 1) * HEAD_SIZE]
                for h in range(group)
            ],
            axis=0,
        )
        keys = keys_ref[:, :, lanes].reshape(columns, HEAD_SIZE)
        values = values_ref[:, :, lanes].reshape(columns, HEAD_SIZE)
        scores = lax.dot_general(
            stacked.astype(BF16), keys, (((1,), (1,)), ((), ())), preferred_element_type=F32
        )
        scores = jnp.where(own, scores * scaling, -1e30)
        new_key = jnp.concatenate([new_key_ref[:, lanes].astype(F32)] * group, axis=0)
        new_value = jnp.concatenate([new_value_ref[:, lanes].astype(F32)] * group, axis=0)
        new_score = jnp.sum(stacked * new_key, axis=1, keepdims=True) * scaling
        top = jnp.maximum(jnp.max(scores, axis=1, keepdims=True), new_score)
        weights = jnp.exp(scores - top)
        new_weight = jnp.exp(new_score - top)
        total = jnp.sum(weights, axis=1, keepdims=True) + new_weight
        probs = (weights / total).astype(BF16)
        new_prob = (new_weight / total).astype(BF16).astype(F32)
        attended = jnp.dot(probs, values, preferred_element_type=F32) + new_prob * new_value
        pieces += [attended[h * ROWS : (h + 1) * ROWS] for h in range(group)]
    resid = hidden_ref[...].astype(F32) + jnp.concatenate(pieces, axis=1)
    meansq = jnp.mean(resid * resid, axis=1, keepdims=True)
    return resid * lax.rsqrt(meansq + epsilon) * gain_ref[...]


def slot_weights(routes_ref, chips, my_plane, my_place):
    slots = chips * BLOCK
    levels = chips // PLANE
    place = lax.broadcasted_iota(jnp.int32, (ROWS, slots), 1)
    token = lax.broadcasted_iota(jnp.int32, (ROWS, slots), 0)
    expert = my_plane * PLANE + (place // (BLOCK * levels) + my_place) % PLANE
    expert = expert.astype(F32)
    level = (place // BLOCK) % levels
    quarter = 2 * ((place // 8) % 2) + ((place // 4) % 2 + (place // BLOCK) % 2) % 2
    picked, mixed = [], []
    for j in range(levels):
        ids, weights = routes_ref[j, 0:ROWS, :], routes_ref[j, ROWS : 2 * ROWS, :]
        chosen = jnp.zeros((ROWS, slots), F32)
        weight = jnp.zeros((ROWS, slots), F32)
        for k in range(ROWS):
            hit = ids[:, k : k + 1] == expert
            chosen = jnp.where(hit, 1.0, chosen)
            weight = jnp.where(hit, weights[:, k : k + 1], weight)
        rank = jnp.zeros((ROWS, slots), F32)
        for t in range(ROWS - 1):
            rank = rank + jnp.where(token > t, chosen[t : t + 1, :], 0.0)
        live = jnp.where(rank == (place % CAPACITY).astype(F32), chosen, 0.0)
        live = jnp.where(level == j, live, 0.0)
        picked += [jnp.where(quarter == q, live, 0.0) for q in range(4)]
        mixed += [jnp.where(quarter == q, live * weight, 0.0) for q in range(4)]
    return jnp.concatenate(picked, axis=0), jnp.concatenate(mixed, axis=0)


def layer_kernel(
    chips,
    hidden_hbm,
    query_hbm,
    keys_hbm,
    values_hbm,
    new_key_hbm,
    new_value_hbm,
    gain_hbm,
    ids_hbm,
    gates_hbm,
    gate_hbm,
    up_hbm,
    down_hbm,
    out_ref,
    hidden_ref,
    query_ref,
    keys_ref,
    values_ref,
    new_key_ref,
    new_value_ref,
    gain_ref,
    ids_ref,
    gates_ref,
    gate,
    up,
    down,
    routes,
    line_rows,
    outgoing,
    arrived,
    row_buffer,
    gated,
    raised,
    activated,
    mine,
    give,
    take,
    replies,
    answers,
    mixed,
    sums_out,
    sums_in,
    own_sums,
    input_sem,
    weight_sem,
    route_send,
    route_recv,
    line_send,
    line_recv,
    sum_send,
    sum_recv,
    send_sem,
    recv_sem,
    pass_send,
    pass_recv,
    swap_send,
    swap_recv,
    reply_send,
    reply_recv,
):
    width = hidden_ref.shape[1]
    part = width // PARTS
    quarter = part // 4
    plane_rows = chips * CAPACITY
    levels = chips // PLANE
    group_rows = levels * BLOCK
    line = 4 * ROWS
    me = lax.axis_index("ep")
    my_chip, core = me // 2, me % 2
    my_plane, my_place = my_chip // PLANE, my_chip % PLANE
    sibling = my_chip * 2 + (1 - core)

    staged = (
        (query_hbm, query_ref),
        (keys_hbm, keys_ref),
        (values_hbm, values_ref),
        (new_key_hbm, new_key_ref),
        (new_value_hbm, new_value_ref),
        (hidden_hbm, hidden_ref),
        (gain_hbm, gain_ref),
        (ids_hbm, ids_ref),
        (gates_hbm, gates_ref),
    )
    input_copies = [
        pltpu.make_async_copy(source, target, input_sem.at[i])
        for i, (source, target) in enumerate(staged)
    ]
    for copy in input_copies:
        copy.start()
    weight_copies = [
        pltpu.make_async_copy(source.at[0], target, weight_sem.at[i])
        for i, (source, target) in enumerate(((gate_hbm, gate), (up_hbm, up), (down_hbm, down)))
    ]
    for copy in weight_copies:
        copy.start()

    def beside(offset):
        return {"ep": (my_plane * PLANE + (my_place + offset) % PLANE) * 2 + core}

    def along(offset):
        return {"ep": (((my_plane + offset) % levels) * PLANE + my_place) * 2 + core}

    barrier = pltpu.get_barrier_semaphore()
    mesh_ids = pl.DeviceIdType.MESH
    for j in range(1, levels):
        pl.semaphore_signal(barrier, inc=1, device_id=along(j), device_id_type=mesh_ids)
    for k in range(1, PLANE):
        pl.semaphore_signal(barrier, inc=1, device_id=beside(k), device_id_type=mesh_ids)
    pl.semaphore_signal(barrier, inc=1, device_id={"ep": sibling}, device_id_type=mesh_ids)

    def send(source, target, send_flag, recv_flag, device):
        return pltpu.make_async_remote_copy(
            src_ref=source,
            dst_ref=target,
            send_sem=send_flag,
            recv_sem=recv_flag,
            device_id=device,
            device_id_type=mesh_ids,
        )

    def group(k):
        return slice(k * group_rows, (k + 1) * group_rows)

    def lines(j):
        return slice(j * line, (j + 1) * line)

    def route(j):
        return send(routes.at[0], routes.at[j], route_send.at[j], route_recv.at[j], along(j))

    def spread_row(h, j):
        return send(
            line_rows.at[h, lines(0)],
            line_rows.at[h, lines(j)],
            line_send.at[h, j],
            line_recv.at[h, j],
            along(j),
        )

    def dispatch(h, k):
        return send(
            outgoing.at[h, group(k)],
            arrived.at[h, 0, group(k)],
            send_sem.at[h, k],
            recv_sem.at[h, k],
            beside(k),
        )

    def pass_on(h, k):
        return send(
            arrived.at[h, 0, group(k)],
            arrived.at[h, 1, group(k)],
            pass_send.at[h, k],
            pass_recv.at[h, k],
            {"ep": sibling},
        )

    def reply(h, k):
        return send(
            replies.at[h, group(k)],
            answers.at[h, group(k)],
            reply_send.at[h, k],
            reply_recv.at[h, k],
            beside(PLANE - k),
        )

    def send_sum(h, j):
        return send(
            sums_out.at[h, lines(j)],
            sums_in.at[h, lines(j)],
            sum_send.at[h, j],
            sum_recv.at[h, j],
            along(levels - j),
        )

    for copy in input_copies:
        copy.wait()
    routes[0] = jnp.zeros(routes.shape[1:], F32)
    routes[0, 0:ROWS, 0 : ids_ref.shape[1]] = ids_ref[...].astype(F32)
    routes[0, ROWS : 2 * ROWS, 0 : gates_ref.shape[1]] = gates_ref[...]
    normed = attention_rows(
        hidden_ref, query_ref, keys_ref, values_ref, new_key_ref, new_value_ref, gain_ref
    )
    for h in range(PARTS):
        line_rows[h, lines(0)] = jnp.concatenate(
            [normed[:, h * part + q * quarter : h * part + (q + 1) * quarter] for q in range(4)],
            axis=0,
        ).astype(BF16)
    pl.semaphore_wait(barrier, levels + PLANE - 1)
    for j in range(1, levels):
        route(j).start()
    for j in range(1, levels):
        spread_row(0, j).start()

    def swap(h):
        return pltpu.make_async_remote_copy(
            src_ref=give.at[h],
            dst_ref=take.at[h],
            send_sem=swap_send.at[h],
            recv_sem=swap_recv.at[h],
            device_id={"ep": sibling},
            device_id_type=pl.DeviceIdType.MESH,
        )

    for j in range(1, levels):
        route(j).wait_recv()
    picker, mixing = slot_weights(routes, chips, my_plane, my_place)
    picker = picker.T.astype(BF16)
    mixed[...] = mixing

    def pack(h):
        for j in range(1, levels):
            spread_row(h, j).wait_send()
        if h + 1 < PARTS:
            for j in range(1, levels):
                spread_row(h + 1, j).start()
        for j in range(1, levels):
            spread_row(h, j).wait_recv()
        packed = jnp.dot(picker, line_rows[h], preferred_element_type=F32).astype(BF16)
        outgoing[h] = packed
        arrived[h, 0, group(0)] = packed[group(0)]
        for k in range(1, PLANE):
            dispatch(h, k).start()
        pass_on(h, 0).start()

    pack(0)
    low = lax.broadcasted_iota(jnp.int32, (chips // 2, 8, quarter), 1) < 4

    def swap_halves(x):
        return pltpu.roll(x, 4, axis=1)

    for h in range(PARTS):
        if h + 1 < PARTS:
            pack(h + 1)
        for k in range(1, PLANE):
            dispatch(h, k).wait_recv()
            pass_on(h, k).start()
        for plane in range(2):
            if plane == 1:
                for k in range(PLANE):
                    pass_on(h, k).wait_recv()
            tiles = arrived[h, plane].astype(F32).reshape(chips // 2, 2, 2, 8, quarter)
            for p in range(2):
                a, b = tiles[:, 0, p], tiles[:, 1, p]
                first = jnp.where(low, a, b)
                second = swap_halves(jnp.where(low, b, a))
                for q, x in ((2 * p, first), (2 * p + 1, second)):
                    row_buffer[
                        plane * plane_rows : (plane + 1) * plane_rows,
                        h * part + q * quarter : h * part + (q + 1) * quarter,
                    ] = x.reshape(plane_rows, quarter).astype(BF16)
        if h == 0:
            weight_copies[0].wait()
            weight_copies[1].wait()
        x = row_buffer[:, h * part : (h + 1) * part]
        gate_part = jnp.dot(x, gate[h * part : (h + 1) * part, :], preferred_element_type=F32)
        up_part = jnp.dot(x, up[h * part : (h + 1) * part, :], preferred_element_type=F32)
        if h == 0:
            gated[...] = gate_part
            raised[...] = up_part
        else:
            gated[...] += gate_part
            raised[...] += up_part

    activated[...] = (jax.nn.silu(gated[...]) * raised[...]).astype(BF16)
    weight_copies[2].wait()
    for h in range(PARTS):
        for q in range(4):
            columns = slice(h * part + q * quarter, h * part + (q + 1) * quarter)
            y = jnp.dot(activated[...], down[:, columns], preferred_element_type=F32)
            mine[:, columns] = y[:plane_rows]
            give[h, :, q * quarter : (q + 1) * quarter] = y[plane_rows:].astype(BF16)
        swap(h).start()
    mixing = mixed[...]
    high = mixing.astype(BF16)
    rest = mixing - high.astype(F32)
    middle = rest.astype(BF16)
    last = (rest - middle.astype(F32)).astype(BF16)

    def combine(h):
        for k in range(1, PLANE):
            reply(h, k).wait_recv()
        got = answers[h]
        total = jnp.dot(high, got, preferred_element_type=F32)
        total = total + jnp.dot(middle, got, preferred_element_type=F32)
        total = total + jnp.dot(last, got, preferred_element_type=F32)
        own_sums[h] = total[lines(0)]
        sums_out[h] = total.astype(BF16)
        for j in range(1, levels):
            send_sum(h, j).start()

    for h in range(PARTS):
        swap(h).wait_recv()
        halves = []
        for p in range(2):
            y = []
            for q in (2 * p, 2 * p + 1):
                columns = slice(h * part + q * quarter, h * part + (q + 1) * quarter)
                whole = mine[:, columns] + take[h, :, q * quarter : (q + 1) * quarter].astype(F32)
                y.append(whole.reshape(chips // 2, 8, quarter))
            turned = swap_halves(y[1])
            halves.append((jnp.where(low, y[0], turned), jnp.where(low, turned, y[0])))
        for m in range(chips // 2):
            for side in range(2):
                start = (2 * m + side) * BLOCK
                replies[h, start : start + BLOCK] = jnp.concatenate(
                    [halves[0][side][m], halves[1][side][m]], axis=0
                ).astype(BF16)
        answers[h, group(0)] = replies[h, group(0)]
        if h > 0:
            for k in range(1, PLANE):
                reply(h - 1, k).wait_send()
        for k in range(1, PLANE):
            reply(h, k).start()
        if h > 0:
            combine(h - 1)

    combine(PARTS - 1)
    for h in range(PARTS):
        total = own_sums[h]
        for j in range(1, levels):
            send_sum(h, j).wait_recv()
            total = total + sums_in[h, lines(j)].astype(F32)
        for q in range(4):
            columns = slice(h * part + q * quarter, h * part + (q + 1) * quarter)
            out_ref[:, columns] = total[q * ROWS : (q + 1) * ROWS].astype(out_ref.dtype)

    for j in range(1, levels):
        route(j).wait_send()
    for k in range(1, PLANE):
        reply(PARTS - 1, k).wait_send()
    for h in range(PARTS):
        for j in range(1, levels):
            send_sum(h, j).wait_send()
        for k in range(1, PLANE):
            dispatch(h, k).wait_send()
        for k in range(PLANE):
            pass_on(h, k).wait_send()
        swap(h).wait_send()


def fused_layer(
    hidden,
    query,
    cached_key_store,
    cached_value_store,
    current_key,
    current_value,
    norm_gain,
    expert_ids,
    gate_weights,
    w_gate,
    w_up,
    w_down,
):
    chips = lax.axis_size("ep") // 2
    width = hidden.shape[1]
    part = width // PARTS
    slots = chips * BLOCK
    units = w_gate.shape[2]
    pair_rows = 2 * chips * CAPACITY
    levels = chips // PLANE
    line_rows = levels * 4 * ROWS
    small = (
        hidden,
        query,
        cached_key_store,
        cached_value_store,
        current_key,
        current_value,
        norm_gain.reshape(1, width),
        expert_ids,
        gate_weights,
    )
    dma = pltpu.SemaphoreType.DMA
    vmem = pl.BlockSpec(memory_space=pltpu.VMEM)
    hbm = pl.BlockSpec(memory_space=pltpu.HBM)
    return pl.pallas_call(
        functools.partial(layer_kernel, chips),
        out_shape=jax.ShapeDtypeStruct(hidden.shape, BF16),
        in_specs=[hbm] * 12,
        out_specs=vmem,
        scratch_shapes=[pltpu.VMEM(x.shape, x.dtype) for x in small]
        + [
            pltpu.VMEM((width, units), BF16),
            pltpu.VMEM((width, units), BF16),
            pltpu.VMEM((units, width), BF16),
            pltpu.VMEM((levels, 2 * ROWS, 128), F32),
            pltpu.VMEM((PARTS, line_rows, part // 4), BF16),
            pltpu.VMEM((PARTS, slots, part // 4), BF16),
            pltpu.VMEM((PARTS, 2, slots, part // 4), BF16),
            pltpu.VMEM((pair_rows, width), BF16),
            pltpu.VMEM((pair_rows, units), F32),
            pltpu.VMEM((pair_rows, units), F32),
            pltpu.VMEM((pair_rows, units), BF16),
            pltpu.VMEM((pair_rows // 2, width), F32),
            pltpu.VMEM((PARTS, pair_rows // 2, part), BF16),
            pltpu.VMEM((PARTS, pair_rows // 2, part), BF16),
            pltpu.VMEM((PARTS, slots, part // 4), BF16),
            pltpu.VMEM((PARTS, slots, part // 4), BF16),
            pltpu.VMEM((line_rows, slots), F32),
            pltpu.VMEM((PARTS, line_rows, part // 4), BF16),
            pltpu.VMEM((PARTS, line_rows, part // 4), BF16),
            pltpu.VMEM((PARTS, 4 * ROWS, part // 4), F32),
            dma((9,)),
            dma((3,)),
            dma((levels,)),
            dma((levels,)),
            dma((PARTS, levels)),
            dma((PARTS, levels)),
            dma((PARTS, levels)),
            dma((PARTS, levels)),
            dma((PARTS, PLANE)),
            dma((PARTS, PLANE)),
            dma((PARTS, PLANE)),
            dma((PARTS, PLANE)),
            dma((PARTS,)),
            dma((PARTS,)),
            dma((PARTS, PLANE)),
            dma((PARTS, PLANE)),
        ],
        compiler_params=pltpu.CompilerParams(
            collective_id=0, has_side_effects=True, vmem_limit_bytes=62 * 1024 * 1024
        ),
        cost_estimate=pl.CostEstimate(
            flops=6 * pair_rows * width * units,
            bytes_accessed=6 * width * units,
            transcendentals=pair_rows * units,
        ),
    )(*small, w_gate, w_up, w_down)


def takes_fused_layer(row_count, chosen_count, units):
    if lax.axis_size("sub") != 1 or lax.axis_size("group") != 1 or 2 * units != FF:
        return False
    chips = lax.axis_size("ep") // 2
    if row_count != ROWS or chosen_count != ROWS or chips % PLANE != 0:
        return False
    return chips * CAPACITY == row_count * chosen_count


def shards(
    hidden,
    query,
    cached_key_store,
    cached_value_store,
    current_key,
    current_value,
    norm_gain,
    expert_ids,
    gate_weights,
    w_gate,
    w_up,
    w_down,
):
    ep_count = lax.axis_size("ep")
    sub_count = lax.axis_size("sub")
    sub_place = lax.axis_index("sub")
    count_of_rows = hidden.shape[0]
    if takes_fused_layer(hidden.shape[0], expert_ids.shape[1], w_gate.shape[2]):
        return fused_layer(
            hidden,
            query,
            cached_key_store,
            cached_value_store,
            current_key,
            current_value,
            norm_gain,
            expert_ids,
            gate_weights,
            w_gate,
            w_up,
            w_down,
        )
    chosen_count = expert_ids.shape[1]
    slice_units = sub_count * w_gate.shape[2]
    spread = FF // slice_units
    experts = ep_count // spread
    capacity = max(2, count_of_rows * chosen_count // experts)
    ids_pair = expert_ids.reshape(sub_count, count_of_rows, chosen_count)
    gates_pair = gate_weights.reshape(sub_count, count_of_rows, chosen_count)
    normed = attend_norm(
        hidden, query, cached_key_store, cached_value_store, current_key, current_value, norm_gain
    )
    merged = moe_block(
        normed, ids_pair, gates_pair, w_gate, w_up, w_down, experts, spread, capacity, sub_place
    )
    return merged.reshape(sub_count * count_of_rows, merged.shape[2])


def solution(mesh):
    return jax.shard_map(
        shards,
        mesh=mesh,
        in_specs=(
            P(("group", "ep", "sub"), None),
            P(("group", "ep", "sub"), None),
            P(("group", "ep", "sub"), None, None),
            P(("group", "ep", "sub"), None, None),
            P(("group", "ep", "sub"), None),
            P(("group", "ep", "sub"), None),
            P(),
            P(("group", "ep"), None),
            P(("group", "ep"), None),
            P("ep", None, "sub"),
            P("ep", None, "sub"),
            P("ep", None, "sub"),
        ),
        out_specs=P(("group", "ep"), "sub"),
        check_vma=False,
    )
```
